512 devices in a mesh: dp: 128 (over y, z_hi, x), head: 4 (over z_lo, core).
Axes of the slice: x: 4, y: 8, z: 8 (z_hi: 4, z_lo: 2; z = z_hi * 2 + z_lo), core: 2. Of those that a mesh axis runs over, the one named last changes fastest.
Arguments:
- trunk: bfloat16 [22528, 4096], P(('dp', 'head')), may hold values from -6 to 6
- keys: bfloat16 [4, 22528, 4096], P('head', 'dp'), may hold values from -900 to 900
- gains: float32 [4, 4096], P('head'), may hold values from 0.1 to 1.9
- grad_out: bfloat16 [4, 22528, 4096], P('head', 'dp'), may hold values from -6 to 6
Outputs:
- grad_trunk: bfloat16 [22528, 4096], P(('dp', 'head'))
- grad_keys: bfloat16 [4, 22528, 4096], P('head', 'dp')
- grad_gains: float32 [4, 4096], P('head')
The draws below stay inside these ranges and needn't reach their ends.
All inputs are finite; a program needn't handle non-finite values.
Results may differ from the reference program's by a relative error of at most 0.012.
The reference program's roundings to bfloat16 on the way (of `queries` and `dscore`) count: a program that leaves them out, or rounds other values in their place, can miss the bound.
Values may be sent and summed in bfloat16 or wider, within the bound.
No kernel may reach another device: no remote copies, remote signals or barrier semaphores. Data moves between devices by JAX's collectives and lax.ppermute only.
A program may use at most 64 MiB of HBM per device.

```python
import jax
import jax.numpy as jnp
from jax import lax

D = 4096
NH = 32
HEAD_DIM = 128
LEN = 176
MTP = 4
TOKENS = 22528


def draw_keys(key, part):
    key = jax.random.fold_in(key, 11)
    first = jax.random.fold_in(key, 0)
    base = jnp.clip(jax.random.normal(first, (MTP, TOKENS, D), jnp.float32), -6.0, 6.0)
    return base.astype(jnp.bfloat16)


def steps_of(own_key, dims, cuts, least, high):
    loudness, own = 1.0, jax.random.fold_in(own_key, 6)
    for dim, blocks in cuts:
        heights = jnp.exp(jax.random.uniform(jax.random.fold_in(own, dim), (blocks,), jnp.float32, least / len(cuts), high / len(cuts)))
        loudness = loudness * jnp.repeat(heights, dims[dim] // blocks).reshape([-1 if axis == dim else 1 for axis in range(len(dims))])
    return loudness


def noise(key, extent, scale, bound, shards=(), held_as=jnp.bfloat16):
    drawn = scale * jax.random.normal(key, extent, jnp.float32)
    if shards:
        drawn = drawn * steps_of(key, extent, shards, -0.22, 0.18)
    return jnp.clip(drawn, -bound, bound).astype(held_as)


def setup_inputs(seed: int = 0) -> dict:
    key_list = jax.random.split(jax.random.key(seed), 5)
    return {
        "trunk": noise(key_list[0], (TOKENS, D), 1.0, 6.0, ((0, 512),)),
        "keys": draw_keys(jax.random.fold_in(key_list[4], 71), 0),
        "gains": jnp.clip(1.0 + 0.18 * jax.random.normal(key_list[2], (MTP, D), jnp.float32), 0.1, 1.9),
        "grad_out": noise(key_list[3], (MTP, TOKENS, D), 1.0, 6.0, ((0, 4), (1, 128))),
    }


def one_sequence(rows, keyset, cotan, gain):
    length = rows.shape[0]
    scale = jnp.float32(HEAD_DIM ** (-0.5))
    xf = rows.astype(jnp.float32)
    rscale = lax.rsqrt(lax.optimization_barrier(jnp.mean(xf * xf, axis=-1, keepdims=True)) + 1e-05)
    normed = xf * rscale
    queries = (normed * gain).astype(jnp.bfloat16)
    qf = queries.astype(jnp.float32).reshape(length, NH, HEAD_DIM)
    kf = keyset.astype(jnp.float32).reshape(length, NH, HEAD_DIM)
    cf = cotan.astype(jnp.float32).reshape(length, NH, HEAD_DIM)
    scores = jnp.einsum('qhd,khd->hqk', qf, kf) * scale
    upper = jnp.arange(length)[:, None] >= jnp.arange(length)[None, :]
    scores = jnp.where(upper[None], scores, -jnp.inf)
    top = lax.optimization_barrier(jnp.max(scores, axis=-1, keepdims=True))
    expo = jnp.exp(scores - top)
    probs = expo / lax.optimization_barrier(jnp.sum(expo, axis=-1, keepdims=True))
    dprob = jnp.einsum('qhd,khd->hqk', cf, qf)
    delta = lax.optimization_barrier(jnp.sum(probs * dprob, axis=-1, keepdims=True))
    dscore = (probs * (dprob - delta)).astype(jnp.bfloat16).astype(jnp.float32)
    pround = probs.astype(jnp.bfloat16).astype(jnp.float32)
    dquery = jnp.einsum('hqk,khd->qhd', dscore, kf) * scale
    dkey = (jnp.einsum('hqk,qhd->khd', dscore, qf) * scale).reshape(length, D).astype(jnp.bfloat16)
    dvalue = jnp.einsum('hqk,qhd->khd', pround, cf)
    dnorm = (dquery + dvalue).reshape(length, D)
    gain_term = lax.optimization_barrier(jnp.sum(normed * dnorm, axis=0))
    weighted = gain * dnorm
    term = rscale * (weighted - normed * lax.optimization_barrier(jnp.mean(weighted * normed, axis=-1, keepdims=True)))
    return (term, dkey, gain_term)

def reference(trunk, keys, gains, grad_out):
    nseq = trunk.shape[0] // LEN
    rows = trunk.reshape(nseq, LEN, D)
    total = jnp.zeros((nseq, LEN, D), jnp.float32)
    dkeys = []
    dgains = []
    for head in range(MTP):
        keyset = keys[head].reshape(nseq, LEN, D)
        cotan = grad_out[head].reshape(nseq, LEN, D)
        gain = gains[head]

        def step(items):
            return one_sequence(items[0], items[1], items[2], gain)
        term, dkey, gain_term = lax.map(step, (rows, keyset, cotan))
        total = total + term
        dkeys.append(dkey.reshape(nseq * LEN, D))
        dgains.append(lax.optimization_barrier(jnp.sum(gain_term, axis=0)))
    grad_trunk = total.reshape(nseq * LEN, D).astype(jnp.bfloat16)
    return (grad_trunk, jnp.stack(dkeys), jnp.stack(dgains))
```

```python
import functools
import math

import jax
import jax.numpy as jnp
from jax import lax
from jax.experimental import pallas as pl
from jax.experimental.pallas import tpu as pltpu
from jax.sharding import Mesh
from jax.sharding import PartitionSpec as P

NH = 32
HEAD_DIM = 128
BF = jnp.bfloat16
F32 = jnp.float32
NT = (((1,), (1,)), ((), ()))
TN = (((0,), (0,)), ((), ()))
HEAD = ("zl", "core")
LIMIT = 48 * 1024 * 1024


def attention_kernel(peers, own, core, far, farcore, keys_hbm, cot_hbm, gain_ref, gk_ref, give_ref, keep_ref, gterm_ref,
                     xf, w, rs, macc, gsum, keys, cot, sems):
    part = own.shape[0]
    length, width = xf.shape
    fetch_k = pltpu.make_async_copy(keys_hbm.at[0], keys, sems.at[0])
    fetch_g = pltpu.make_async_copy(cot_hbm.at[0], cot, sems.at[1])
    fetch_k.start()
    fetch_g.start()
    zl = lax.axis_index("zl")
    c = lax.axis_index("core")

    def columns(a):
        return pl.ds(pl.multiple_of(a * HEAD_DIM, HEAD_DIM), HEAD_DIM)

    for zi in range(2):
        for ci in range(2):

            @pl.when((zl == zi) & (c == ci))
            def _(zi=zi, ci=ci):
                here = 2 * part * zi
                there = 2 * part * (1 - zi)
                for ref, base, which in ((own, here, ci), (core, here, 1 - ci), (far, there, ci), (farcore, there, 1 - ci)):
                    start = base + part * which

                    def put(a, _, ref=ref, start=start):
                        sl = columns(a)
                        xf[pl.ds(start, part), sl] = ref[:, sl].astype(F32)
                        return 0

                    lax.fori_loop(0, width // HEAD_DIM, put, 0, unroll=4)

    def square(a, acc):
        v = xf[:, columns(a)]
        return acc + v * v

    total = lax.fori_loop(0, width // HEAD_DIM, square, jnp.zeros((length, HEAD_DIM), F32), unroll=2)
    mean = jnp.sum(total, axis=-1, keepdims=True) * (1.0 / width)
    rs[...] = jnp.broadcast_to(lax.rsqrt(mean + 1e-05), rs.shape)
    macc[...] = jnp.zeros_like(macc)
    fetch_k.wait()
    fetch_g.wait()
    scale = F32(HEAD_DIM ** (-0.5))
    scale2 = F32(HEAD_DIM ** (-0.5) * math.log2(math.e))

    def head(a, _):
        sl = columns(a)
        normed = xf[:, sl] * rs[...]
        gain = gain_ref[:, sl]
        q = (normed * gain).astype(BF)
        k = keys[:, sl]
        g = cot[:, sl]
        st = lax.dot_general(k, q, NT, preferred_element_type=F32)
        dpt = lax.dot_general(q, g, NT, preferred_element_type=F32)
        cols = lax.broadcasted_iota(jnp.int32, st.shape, 1)
        rows = lax.broadcasted_iota(jnp.int32, st.shape, 0)
        st = jnp.where(rows <= cols, st, -jnp.inf)
        top = jnp.max(st, axis=0, keepdims=True)
        e = jnp.exp2((st - top) * scale2)
        p = e * (1.0 / jnp.sum(e, axis=0, keepdims=True))
        pd = p * dpt
        delta = jnp.sum(pd, axis=0, keepdims=True)
        dst = (pd - p * delta).astype(BF)
        pb = p.astype(BF)
        dv = jnp.dot(pb, g, preferred_element_type=F32)
        dk = jnp.dot(dst, q, preferred_element_type=F32)
        dq = lax.dot_general(dst, k, TN, preferred_element_type=F32)
        gk_ref[0, :, sl] = (dk * scale).astype(BF)
        dn = dq * scale + dv
        nd = normed * dn
        gsum[pl.ds(a, 1), :] = jnp.sum(nd, axis=0, keepdims=True)
        macc[...] += nd * gain
        w[:, sl] = gain * dn
        return 0

    lax.fori_loop(0, NH, head, 0)
    for i in range(peers):
        gterm_ref[i] = gsum[...].astype(BF)
    r = rs[...]
    m = jnp.sum(macc[...], axis=-1, keepdims=True) * (1.0 / width)
    macc[...] = r * r * m
    for ci in range(2):

        @pl.when(c == ci)
        def _(ci=ci):
            def finish(a, _):
                sl = columns(a)
                term = rs[...] * w[:, sl] - macc[...] * xf[:, sl]
                for zi in range(2):
                    mine = part * (2 * zi + ci)
                    other = part * (2 * zi + 1 - ci)
                    keep_ref[zi, :, sl] = term[mine : mine + part]
                    give_ref[zi, :, sl] = term[other : other + part].astype(BF)
                return 0

            lax.fori_loop(0, width // HEAD_DIM, finish, 0)


def add_kernel(keep, got, mine_ref, send_ref):
    zl = lax.axis_index("zl")
    mine_ref[...] = keep[zl] + got[zl].astype(F32)
    send_ref[...] = (keep[1 - zl] + got[1 - zl].astype(F32)).astype(BF)


def final_kernel(mine, got, out):
    out[...] = (mine[...] + got[...].astype(F32)).astype(BF)


def spread_kernel(peers, got, out):
    total = jnp.sum(got[...].astype(F32), axis=0).astype(BF)
    for i in range(peers):
        out[i] = total


def total_kernel(got, out):
    total = jnp.sum(got[...].astype(F32), axis=0)
    for r in range(total.shape[0]):
        out[0:1, r * HEAD_DIM : (r + 1) * HEAD_DIM] = total[r : r + 1, :]


def swap(v, bit):
    return lax.ppermute(v, HEAD, [(i, i ^ bit) for i in range(4)])


def call(kernel, outs, *args, name, **more):
    return pl.pallas_call(
        kernel,
        out_shape=outs,
        in_specs=[pl.BlockSpec(memory_space=pltpu.VMEM)] * len(args),
        out_specs=jax.tree.map(lambda _: pl.BlockSpec(memory_space=pltpu.VMEM), outs),
        compiler_params=pltpu.CompilerParams(vmem_limit_bytes=LIMIT),
        name=name,
        **more,
    )(*args)


def on_device(near, rest, trunk, keys, gains, grad_out):
    part, width = trunk.shape
    length = keys.shape[1]
    shape = jax.ShapeDtypeStruct
    far = swap(trunk, 2)
    core = swap(trunk, 1)
    farcore = swap(far, 1)
    vmem = pl.BlockSpec(memory_space=pltpu.VMEM)
    hbm = pl.BlockSpec(memory_space=pl.ANY)
    grad_keys, give, keep, gterm = pl.pallas_call(
        functools.partial(attention_kernel, near),
        out_shape=(
            shape((1, length, width), BF),
            shape((2, part, width), BF),
            shape((2, part, width), F32),
            shape((near, NH, HEAD_DIM), BF),
        ),
        in_specs=[vmem] * 4 + [hbm] * 2 + [vmem],
        out_specs=(vmem,) * 4,
        scratch_shapes=[
            pltpu.VMEM((length, width), F32),
            pltpu.VMEM((length, width), F32),
            pltpu.VMEM((length, HEAD_DIM), F32),
            pltpu.VMEM((length, HEAD_DIM), F32),
            pltpu.VMEM((NH, HEAD_DIM), F32),
            pltpu.VMEM((length, width), BF),
            pltpu.VMEM((length, width), BF),
            pltpu.SemaphoreType.DMA((2,)),
        ],
        compiler_params=pltpu.CompilerParams(vmem_limit_bytes=LIMIT),
        name="attention_backward",
    )(trunk, core, far, farcore, keys, grad_out, gains)
    got = swap(give, 1)
    first = lax.all_to_all(gterm, "x", 0, 0, tiled=True)
    mine, send = call(add_kernel, (shape((part, width), F32), shape((part, width), BF)), keep, got, name="add_core")
    last = swap(send, 2)
    wide = call(functools.partial(spread_kernel, rest), shape((rest, NH, HEAD_DIM), BF), first, name="sum_near")
    second = lax.all_to_all(wide, ("y", "zh"), 0, 0, tiled=True)
    grad_trunk = call(final_kernel, shape((part, width), BF), mine, last, name="add_far")
    grad_gains = call(total_kernel, shape((1, width), F32), second, name="sum_rest")
    return grad_trunk, grad_keys, grad_gains


def solution(mesh):
    dp = mesh.shape["dp"]
    near = min(dp, 4)
    zh = 4 if dp >= 16 else 1
    y = dp // near // zh
    fine = Mesh(mesh.devices.reshape(y, zh, near, 2, 2), ("y", "zh", "x", "zl", "core"))
    dps = ("y", "zh", "x")
    return jax.shard_map(
        functools.partial(on_device, near, dp // near),
        mesh=fine,
        in_specs=(
            P(dps + HEAD, None),
            P(HEAD, dps, None),
            P(HEAD, None),
            P(HEAD, dps, None),
        ),
        out_specs=(P(dps + HEAD, None), P(HEAD, dps, None), P(HEAD, None)),
        check_vma=False,
    )
```

```python
import functools
import math

import jax
import jax.numpy as jnp
from jax import lax
from jax.experimental import pallas as pl
from jax.experimental.pallas import tpu as pltpu
from jax.sharding import Mesh
from jax.sharding import PartitionSpec as P

NH = 32
HEAD_DIM = 128
GROUP = 8
SLAB = 48
BF = jnp.bfloat16
F32 = jnp.float32
NT = (((1,), (1,)), ((), ()))
TN = (((0,), (0,)), ((), ()))
HEAD = ("zl", "core")
LIMIT = 24 * 1024 * 1024


def columns(a):
    return pl.ds(pl.multiple_of(a * HEAD_DIM, HEAD_DIM), HEAD_DIM)


def pair_rows(c, first, second, x_ref, rs_ref, base):
    part, width = first.shape
    for ci in range(2):

        @pl.when(c == ci)
        def _(ci=ci):
            low, high = (first, second) if ci == 0 else (second, first)

            def put(a, acc):
                sl = columns(a)
                v = jnp.concatenate([low[:, sl].astype(F32), high[:, sl].astype(F32)], axis=0)
                x_ref[pl.ds(base, 2 * part), sl] = v
                return acc + v * v

            total = lax.fori_loop(0, width // HEAD_DIM, put, jnp.zeros((2 * part, HEAD_DIM), F32), unroll=4)
            mean = jnp.sum(total, axis=-1, keepdims=True) * (1.0 / width)
            rs_ref[pl.ds(base, 2 * part), :] = jnp.broadcast_to(lax.rsqrt(mean + 1e-05), (2 * part, HEAD_DIM))


def near_kernel(own, core, keys, cot, gain, x_ref, rs_ref):
    pair_rows(lax.axis_index("core"), own, core, x_ref, rs_ref, 0)


def attention_kernel(peers, near, near_rs, far, farcore, keys, cot, gain_ref, gk_ref, give_ref, keep_ref, gterm_ref,
                     xf, w, rs, macc, gsum, bias0, bias1, gk, gsems):
    part = far.shape[0]
    length, width = xf.shape
    zl = lax.axis_index("zl")
    c = lax.axis_index("core")
    here = pl.multiple_of(2 * part * zl, 8)
    there = pl.multiple_of(2 * part * (1 - zl), 8)
    pair_rows(c, far, farcore, xf, rs, there)

    def place(a, _):
        sl = columns(a)
        xf[pl.ds(here, 2 * part), sl] = near[:, sl]
        return 0

    lax.fori_loop(0, width // HEAD_DIM, place, 0, unroll=4)
    rs[pl.ds(here, 2 * part), :] = near_rs[...]
    macc[...] = jnp.zeros_like(macc)
    scale = F32(HEAD_DIM ** (-0.5))
    scale2 = F32(HEAD_DIM ** (-0.5) * math.log2(math.e))
    cut = HEAD_DIM
    tail = length - cut

    def triangle(n):
        rows = lax.broadcasted_iota(jnp.int32, (n, n), 0)
        cols = lax.broadcasted_iota(jnp.int32, (n, n), 1)
        return jnp.where(rows <= cols, F32(0), F32(-jnp.inf))

    bias0[...] = triangle(cut)
    bias1[...] = triangle(tail)

    def softmax(s, d):
        top = jnp.max(s, axis=0, keepdims=True)
        e = jnp.exp2(s * scale2 - top * scale2)
        inv = 1.0 / jnp.sum(e, axis=0, keepdims=True)
        delta = jnp.sum(e * d, axis=0, keepdims=True) * inv
        p = e * inv
        return p.astype(BF), (p * (d - delta)).astype(BF)

    def begin(a):
        sl = columns(a)
        normed = xf[:, sl] * rs[...]
        q = (normed * gain_ref[:, sl]).astype(BF)
        st = lax.dot_general(keys[0, :, sl], q, NT, preferred_element_type=F32)
        dpt = lax.dot_general(q, cot[0, :, sl], NT, preferred_element_type=F32)
        return sl, q, st, dpt

    def middle(sl, q, st, dpt):
        p0, d0 = softmax(st[:cut, :cut] + bias0[...], dpt[:cut, :cut])
        s1 = jnp.concatenate([st[:cut, cut:], st[cut:, cut:] + bias1[...]], axis=0)
        p1, d1 = softmax(s1, dpt[:, cut:])
        none = jnp.zeros((tail, cut), BF)
        pb = jnp.concatenate([jnp.concatenate([p0, none], axis=0), p1], axis=1)
        dst = jnp.concatenate([jnp.concatenate([d0, none], axis=0), d1], axis=1)
        return sl, q, pb, dst

    def end(a, sl, q, pb, dst):
        dv = jnp.dot(pb, cot[0, :, sl], preferred_element_type=F32)
        dk = jnp.dot(dst, q, preferred_element_type=F32)
        dq = lax.dot_general(dst, keys[0, :, sl], TN, preferred_element_type=F32)
        gk[0, :, sl] = (dk * scale).astype(BF)
        dn = dq * scale + dv
        nd = xf[:, sl] * rs[...] * dn
        gain = gain_ref[:, sl]
        gsum[pl.ds(a, 1), :] = jnp.sum(nd, axis=0, keepdims=True)
        w[:, sl] = gain * dn
        return nd * gain

    def send_group(i):
        sl = pl.ds(pl.multiple_of(i * GROUP * HEAD_DIM, GROUP * HEAD_DIM), GROUP * HEAD_DIM)
        return pltpu.make_async_copy(gk.at[0, :, sl], gk_ref.at[0, :, sl], gsems.at[i])

    def heads(i, _):
        first, second, mean = {}, {}, None
        for step in range(GROUP + 2):
            if step < GROUP:
                first[step] = begin(i * GROUP + step)
            if 0 <= step - 1 < GROUP:
                second[step - 1] = middle(*first.pop(step - 1))
            if 0 <= step - 2 < GROUP:
                one = end(i * GROUP + step - 2, *second.pop(step - 2))
                mean = one if mean is None else mean + one
        macc[...] += mean
        send_group(i).start()
        return 0

    lax.fori_loop(0, NH // GROUP, heads, 0)
    for i in range(peers):
        gterm_ref[i] = gsum[...].astype(BF)
    r = rs[...]
    m = jnp.sum(macc[...], axis=-1, keepdims=True) * (1.0 / width)
    macc[...] = r * r * m
    for ci in range(2):

        @pl.when(c == ci)
        def _(ci=ci):
            def finish(a, _):
                sl = columns(a)
                term = rs[...] * w[:, sl] - macc[...] * xf[:, sl]
                for zi in range(2):
                    mine = part * (2 * zi + ci)
                    other = part * (2 * zi + 1 - ci)
                    keep_ref[SLAB * zi : SLAB * zi + part, sl] = term[mine : mine + part]
                    give_ref[SLAB * zi : SLAB * zi + part, sl] = term[other : other + part].astype(BF)
                return 0

            lax.fori_loop(0, width // HEAD_DIM, finish, 0, unroll=2)

    for i in range(NH // GROUP):
        send_group(i).wait()


def spread_kernel(peers, first, wide_ref):
    total = jnp.sum(first[...].astype(F32), axis=0).astype(BF)
    for i in range(peers):
        wide_ref[i] = total


def between_kernel(keep, got, mine_ref, send_ref):
    zl = lax.axis_index("zl")
    here = pl.ds(pl.multiple_of(SLAB * zl, SLAB), SLAB)
    there = pl.ds(pl.multiple_of(SLAB * (1 - zl), SLAB), SLAB)
    mine_ref[...] = keep[here, :] + got[here, :].astype(F32)
    send_ref[:SLAB] = (keep[there, :] + got[there, :].astype(F32)).astype(send_ref.dtype)


def final_kernel(mine, last, second, trunk_ref, gains_ref):
    total = jnp.sum(second[...].astype(F32), axis=0)
    for r in range(total.shape[0]):
        gains_ref[0:1, r * HEAD_DIM : (r + 1) * HEAD_DIM] = total[r : r + 1, :]
    both = mine[...] + last[:SLAB].astype(F32)
    trunk_ref[...] = both[: trunk_ref.shape[0]].astype(BF)


def swap(v, bit):
    return lax.ppermute(v, HEAD, [(i, i ^ bit) for i in range(4)])


def call(kernel, outs, args, name, hbm_in=(), hbm_out=(), scratch=(), cost=(0, 0), limit=LIMIT):
    vmem = pl.BlockSpec(memory_space=pltpu.VMEM)
    hbm = pl.BlockSpec(memory_space=pltpu.HBM)
    return pl.pallas_call(
        kernel,
        out_shape=outs,
        in_specs=[hbm if i in hbm_in else vmem for i in range(len(args))],
        out_specs=tuple(hbm if i in hbm_out else vmem for i in range(len(outs))),
        scratch_shapes=list(scratch),
        compiler_params=pltpu.CompilerParams(vmem_limit_bytes=limit),
        cost_estimate=pl.CostEstimate(flops=cost[0], bytes_accessed=cost[1], transcendentals=0),
        name=name,
    )(*args)


def on_device(near, rest, trunk, keys, gains, grad_out):
    part, width = trunk.shape
    length = keys.shape[1]
    shape = jax.ShapeDtypeStruct
    far = swap(trunk, 2)
    core = swap(trunk, 1)
    x_near, rs_near = call(
        near_kernel,
        (
            shape((2 * part, width), F32),
            shape((2 * part, HEAD_DIM), F32),
        ),
        (trunk, core, keys, grad_out, gains),
        "near_rows",
        cost=(0, 8 << 20),
        limit=24 * 1024 * 1024,
    )
    far, x_near = lax.optimization_barrier((far, x_near))
    farcore = swap(far, 1)
    grad_keys, give, keep, gterm = call(
        functools.partial(attention_kernel, near),
        (
            shape((1, length, width), BF),
            shape((2 * SLAB, width), BF),
            shape((2 * SLAB, width), F32),
            shape((near, NH, HEAD_DIM), BF),
        ),
        (x_near, rs_near, far, farcore, keys, grad_out, gains),
        "attention_backward",
        hbm_out=(0,),
        scratch=[
            pltpu.VMEM((length, width), F32),
            pltpu.VMEM((length, width), F32),
            pltpu.VMEM((length, HEAD_DIM), F32),
            pltpu.VMEM((length, HEAD_DIM), F32),
            pltpu.VMEM((NH, HEAD_DIM), F32),
            pltpu.VMEM((HEAD_DIM, HEAD_DIM), F32),
            pltpu.VMEM((length - HEAD_DIM, length - HEAD_DIM), F32),
            pltpu.VMEM((1, length, width), BF),
            pltpu.SemaphoreType.DMA((NH // GROUP,)),
        ],
        cost=(10 * length * length * width, 16 << 20),
    )
    got = swap(give, 1)
    first = lax.all_to_all(gterm, "zh", 0, 0, tiled=True)
    got, first = lax.optimization_barrier((got, first))
    mine, send = call(
        between_kernel, (shape((SLAB, width), F32), shape((64, width), BF)), (keep, got), "add_core"
    )
    send, first = lax.optimization_barrier((send, first))
    last = swap(send, 2)
    (wide,) = call(
        functools.partial(spread_kernel, rest),
        (shape((rest, NH, HEAD_DIM), BF),),
        (first,),
        "sum_near",
        cost=(8 << 30, 0),
    )
    second = lax.all_to_all(wide, ("y", "x"), 0, 0, tiled=True)
    grad_trunk, grad_gains = call(
        final_kernel, (shape((part, width), BF), shape((1, width), F32)), (mine, last, second), "add_far"
    )
    return grad_trunk, grad_keys, grad_gains


def solution(mesh):
    dp = mesh.shape["dp"]
    near = min(dp, 4)
    zh = 4 if dp >= 16 else 1
    y = dp // near // zh
    fine = Mesh(mesh.devices.reshape(y, zh, near, 2, 2), ("y", "zh", "x", "zl", "core"))
    dps = ("y", "zh", "x")
    return jax.shard_map(
        functools.partial(on_device, zh, dp // zh),
        mesh=fine,
        in_specs=(
            P(dps + HEAD, None),
            P(HEAD, dps, None),
            P(HEAD, None),
            P(HEAD, dps, None),
        ),
        out_specs=(P(dps + HEAD, None), P(HEAD, dps, None), P(HEAD, None)),
        check_vma=False,
    )
```

```python
import functools
import math

import jax
import jax.numpy as jnp
from jax import lax
from jax.experimental import pallas as pl
from jax.experimental.pallas import tpu as pltpu
from jax.sharding import Mesh
from jax.sharding import PartitionSpec as P

NH = 32
HEAD_DIM = 128
GROUP = 16
SLAB = 48
BF = jnp.bfloat16
F32 = jnp.float32
NT = (((1,), (1,)), ((), ()))
TN = (((0,), (0,)), ((), ()))
HEAD = ("zl", "core")
LIMIT = 24 * 1024 * 1024


def columns(a):
    return pl.ds(pl.multiple_of(a * HEAD_DIM, HEAD_DIM), HEAD_DIM)


def pair_rows(c, first, second, x_ref, rs_ref, base):
    part, width = first.shape
    for ci in range(2):

        @pl.when(c == ci)
        def _(ci=ci):
            low, high = (first, second) if ci == 0 else (second, first)

            def put(a, acc):
                sl = columns(a)
                v = jnp.concatenate([low[:, sl].astype(F32), high[:, sl].astype(F32)], axis=0)
                x_ref[pl.ds(base, 2 * part), sl] = v
                return acc + v * v

            total = lax.fori_loop(0, width // HEAD_DIM, put, jnp.zeros((2 * part, HEAD_DIM), F32), unroll=4)
            mean = jnp.sum(total, axis=-1, keepdims=True) * (1.0 / width)
            rs_ref[pl.ds(base, 2 * part), :] = jnp.broadcast_to(lax.rsqrt(mean + 1e-05), (2 * part, HEAD_DIM))


def own_kernel(own, keys, cot, gain, x_ref, rs_ref):
    part, width = own.shape

    def put(a, acc):
        sl = columns(a)
        v = own[:, sl].astype(F32)
        x_ref[:, sl] = v
        return acc + v * v

    total = lax.fori_loop(0, width // HEAD_DIM, put, jnp.zeros((part, HEAD_DIM), F32), unroll=4)
    mean = jnp.sum(total, axis=-1, keepdims=True) * (1.0 / width)
    rs_ref[...] = jnp.broadcast_to(lax.rsqrt(mean + 1e-05), (part, HEAD_DIM))


def attention_kernel(peers, own, own_rs, core, far, farcore, keys, cot, gain_ref, gk_ref, give_ref, keep_ref, gterm_ref,
                     xf, w, rs, macc, gsum, bias0, bias1, gk, gsems):
    part = far.shape[0]
    length, width = xf.shape
    zl = lax.axis_index("zl")
    c = lax.axis_index("core")
    here = pl.multiple_of(2 * part * zl, 8)
    there = pl.multiple_of(2 * part * (1 - zl), 8)
    pair_rows(c, far, farcore, xf, rs, there)
    pair_rows(c, own, core, xf, rs, here)
    macc[...] = jnp.zeros_like(macc)
    scale = F32(HEAD_DIM ** (-0.5))
    scale2 = F32(HEAD_DIM ** (-0.5) * math.log2(math.e))
    cut = HEAD_DIM
    tail = length - cut

    def triangle(n):
        rows = lax.broadcasted_iota(jnp.int32, (n, n), 0)
        cols = lax.broadcasted_iota(jnp.int32, (n, n), 1)
        return jnp.where(rows <= cols, F32(0), F32(-jnp.inf))

    bias0[...] = triangle(cut)
    bias1[...] = triangle(tail)

    def softmax(s, d):
        top = jnp.max(s, axis=0, keepdims=True)
        e = jnp.exp2(s * scale2 - top * scale2)
        inv = 1.0 / jnp.sum(e, axis=0, keepdims=True)
        delta = jnp.sum(e * d, axis=0, keepdims=True) * inv
        p = e * inv
        return p.astype(BF), (p * (d - delta)).astype(BF)

    def begin(a):
        sl = columns(a)
        normed = xf[:, sl] * rs[...]
        q = (normed * gain_ref[:, sl]).astype(BF)
        st = lax.dot_general(keys[0, :, sl], q, NT, preferred_element_type=F32)
        dpt = lax.dot_general(q, cot[0, :, sl], NT, preferred_element_type=F32)
        return sl, q, st, dpt

    def middle(sl, q, st, dpt):
        p0, d0 = softmax(st[:cut, :cut] + bias0[...], dpt[:cut, :cut])
        s1 = jnp.concatenate([st[:cut, cut:], st[cut:, cut:] + bias1[...]], axis=0)
        p1, d1 = softmax(s1, dpt[:, cut:])
        none = jnp.zeros((tail, cut), BF)
        pb = jnp.concatenate([jnp.concatenate([p0, none], axis=0), p1], axis=1)
        dst = jnp.concatenate([jnp.concatenate([d0, none], axis=0), d1], axis=1)
        return sl, q, pb, dst

    def end(a, sl, q, pb, dst):
        dv = jnp.dot(pb, cot[0, :, sl], preferred_element_type=F32)
        dk = jnp.dot(dst, q, preferred_element_type=F32)
        dq = lax.dot_general(dst, keys[0, :, sl], TN, preferred_element_type=F32)
        gk[0, :, sl] = (dk * scale).astype(BF)
        dn = dq * scale + dv
        nd = xf[:, sl] * rs[...] * dn
        gain = gain_ref[:, sl]
        gsum[pl.ds(a, 1), :] = jnp.sum(nd, axis=0, keepdims=True)
        w[:, sl] = gain * dn
        return nd * gain

    def send_group(i):
        sl = pl.ds(pl.multiple_of(i * GROUP * HEAD_DIM, GROUP * HEAD_DIM), GROUP * HEAD_DIM)
        return pltpu.make_async_copy(gk.at[0, :, sl], gk_ref.at[0, :, sl], gsems.at[i])

    def heads(i, _):
        first, second, mean = {}, {}, None
        for step in range(GROUP + 2):
            if step < GROUP:
                first[step] = begin(i * GROUP + step)
            if 0 <= step - 1 < GROUP:
                second[step - 1] = middle(*first.pop(step - 1))
            if 0 <= step - 2 < GROUP:
                one = end(i * GROUP + step - 2, *second.pop(step - 2))
                mean = one if mean is None else mean + one
        macc[...] += mean
        send_group(i).start()
        return 0

    lax.fori_loop(0, NH // GROUP, heads, 0)
    for i in range(peers):
        gterm_ref[i] = gsum[...].astype(BF)
    r = rs[...]
    m = jnp.sum(macc[...], axis=-1, keepdims=True) * (1.0 / width)
    macc[...] = r * r * m
    for ci in range(2):

        @pl.when(c == ci)
        def _(ci=ci):
            def finish(a, _):
                sl = columns(a)
                term = rs[...] * w[:, sl] - macc[...] * xf[:, sl]
                for zi in range(2):
                    mine = part * (2 * zi + ci)
                    other = part * (2 * zi + 1 - ci)
                    keep_ref[SLAB * zi : SLAB * zi + part, sl] = term[mine : mine + part]
                    give_ref[SLAB * zi : SLAB * zi + part, sl] = term[other : other + part].astype(BF)
                return 0

            lax.fori_loop(0, width // HEAD_DIM, finish, 0, unroll=2)

    for i in range(NH // GROUP):
        send_group(i).wait()


def spread_kernel(peers, first, wide_ref):
    total = jnp.sum(first[...].astype(F32), axis=0).astype(BF)
    for i in range(peers):
        wide_ref[i] = total


def between_kernel(keep, got, mine_ref, send_ref):
    zl = lax.axis_index("zl")
    here = pl.ds(pl.multiple_of(SLAB * zl, SLAB), SLAB)
    there = pl.ds(pl.multiple_of(SLAB * (1 - zl), SLAB), SLAB)
    mine_ref[...] = keep[here, :] + got[here, :].astype(F32)
    send_ref[:SLAB] = (keep[there, :] + got[there, :].astype(F32)).astype(send_ref.dtype)


def final_kernel(mine, last, second, trunk_ref, gains_ref):
    total = jnp.sum(second[...].astype(F32), axis=0)
    for r in range(total.shape[0]):
        gains_ref[0:1, r * HEAD_DIM : (r + 1) * HEAD_DIM] = total[r : r + 1, :]
    both = mine[...] + last[:SLAB].astype(F32)
    trunk_ref[...] = both[: trunk_ref.shape[0]].astype(BF)


def swap(v, bit):
    return lax.ppermute(v, HEAD, [(i, i ^ bit) for i in range(4)])


def call(kernel, outs, args, name, hbm_in=(), hbm_out=(), scratch=(), cost=(0, 0), limit=LIMIT):
    vmem = pl.BlockSpec(memory_space=pltpu.VMEM)
    hbm = pl.BlockSpec(memory_space=pltpu.HBM)
    return pl.pallas_call(
        kernel,
        out_shape=outs,
        in_specs=[hbm if i in hbm_in else vmem for i in range(len(args))],
        out_specs=tuple(hbm if i in hbm_out else vmem for i in range(len(outs))),
        scratch_shapes=list(scratch),
        compiler_params=pltpu.CompilerParams(vmem_limit_bytes=limit),
        cost_estimate=pl.CostEstimate(flops=cost[0], bytes_accessed=cost[1], transcendentals=0),
        name=name,
    )(*args)


def on_device(near, rest, trunk, keys, gains, grad_out):
    part, width = trunk.shape
    length = keys.shape[1]
    shape = jax.ShapeDtypeStruct
    far = swap(trunk, 2)
    core = swap(trunk, 1)
    x_own, rs_own = call(
        own_kernel,
        (shape((part, width), F32), shape((part, HEAD_DIM), F32)),
        (trunk, keys, grad_out, gains),
        "own_rows",
        cost=(0, 8 << 20),
        limit=24 * 1024 * 1024,
    )
    far, x_own = lax.optimization_barrier((far, x_own))
    farcore = swap(far, 1)
    grad_keys, give, keep, gterm = call(
        functools.partial(attention_kernel, near),
        (
            shape((1, length, width), BF),
            shape((2 * SLAB, width), BF),
            shape((2 * SLAB, width), F32),
            shape((near, NH, HEAD_DIM), BF),
        ),
        (x_own, rs_own, core, far, farcore, keys, grad_out, gains),
        "attention_backward",
        hbm_out=(0,),
        scratch=[
            pltpu.VMEM((length, width), F32),
            pltpu.VMEM((length, width), F32),
            pltpu.VMEM((length, HEAD_DIM), F32),
            pltpu.VMEM((length, HEAD_DIM), F32),
            pltpu.VMEM((NH, HEAD_DIM), F32),
            pltpu.VMEM((HEAD_DIM, HEAD_DIM), F32),
            pltpu.VMEM((length - HEAD_DIM, length - HEAD_DIM), F32),
            pltpu.VMEM((1, length, width), BF),
            pltpu.SemaphoreType.DMA((NH // GROUP,)),
        ],
        cost=(10 * length * length * width, 16 << 20),
    )
    got = swap(give, 1)
    first = lax.all_to_all(gterm, "zh", 0, 0, tiled=True)
    got, first = lax.optimization_barrier((got, first))
    mine, send = call(
        between_kernel, (shape((SLAB, width), F32), shape((64, width), BF)), (keep, got), "add_core"
    )
    send, first = lax.optimization_barrier((send, first))
    last = swap(send, 2)
    (wide,) = call(
        functools.partial(spread_kernel, rest),
        (shape((rest, NH, HEAD_DIM), BF),),
        (first,),
        "sum_near",
        cost=(8 << 30, 0),
    )
    second = lax.all_to_all(wide, ("y", "x"), 0, 0, tiled=True)
    grad_trunk, grad_gains = call(
        final_kernel, (shape((part, width), BF), shape((1, width), F32)), (mine, last, second), "add_far"
    )
    return grad_trunk, grad_keys, grad_gains


def solution(mesh):
    dp = mesh.shape["dp"]
    near = min(dp, 4)
    zh = 4 if dp >= 16 else 1
    y = dp // near // zh
    fine = Mesh(mesh.devices.reshape(y, zh, near, 2, 2), ("y", "zh", "x", "zl", "core"))
    dps = ("y", "zh", "x")
    return jax.shard_map(
        functools.partial(on_device, zh, dp // zh),
        mesh=fine,
        in_specs=(
            P(dps + HEAD, None),
            P(HEAD, dps, None),
            P(HEAD, None),
            P(HEAD, dps, None),
        ),
        out_specs=(P(dps + HEAD, None), P(HEAD, dps, None), P(HEAD, None)),
        check_vma=False,
    )
```

```python
import functools
import math

import jax
import jax.numpy as jnp
from jax import lax
from jax.experimental import pallas as pl
from jax.experimental.pallas import tpu as pltpu
from jax.sharding import Mesh
from jax.sharding import PartitionSpec as P

NH = 32
HEAD_DIM = 128
GROUP = 32
SLAB = 48
BF = jnp.bfloat16
F32 = jnp.float32
NT = (((1,), (1,)), ((), ()))
TN = (((0,), (0,)), ((), ()))
HEAD = ("zl", "core")
LIMIT = 24 * 1024 * 1024


def columns(a):
    return pl.ds(pl.multiple_of(a * HEAD_DIM, HEAD_DIM), HEAD_DIM)


def pair_rows(c, first, second, x_ref, rs_ref, base):
    part, width = first.shape
    for ci in range(2):

        @pl.when(c == ci)
        def _(ci=ci):
            low, high = (first, second) if ci == 0 else (second, first)

            def put(a, acc):
                sl = columns(a)
                v = jnp.concatenate([low[:, sl].astype(F32), high[:, sl].astype(F32)], axis=0)
                x_ref[pl.ds(base, 2 * part), sl] = v
                return acc + v * v

            total = lax.fori_loop(0, width // HEAD_DIM, put, jnp.zeros((2 * part, HEAD_DIM), F32), unroll=4)
            mean = jnp.sum(total, axis=-1, keepdims=True) * (1.0 / width)
            rs_ref[pl.ds(base, 2 * part), :] = jnp.broadcast_to(lax.rsqrt(mean + 1e-05), (2 * part, HEAD_DIM))


def own_kernel(own, keys, cot, gain, x_ref, rs_ref):
    part, width = own.shape

    def put(a, acc):
        sl = columns(a)
        v = own[:, sl].astype(F32)
        x_ref[:, sl] = v
        return acc + v * v

    total = lax.fori_loop(0, width // HEAD_DIM, put, jnp.zeros((part, HEAD_DIM), F32), unroll=4)
    mean = jnp.sum(total, axis=-1, keepdims=True) * (1.0 / width)
    rs_ref[...] = jnp.broadcast_to(lax.rsqrt(mean + 1e-05), (part, HEAD_DIM))


def near_kernel(own, core, x_ref, rs_ref):
    here = pl.multiple_of(2 * own.shape[0] * lax.axis_index("zl"), 8)
    pair_rows(lax.axis_index("core"), own, core, x_ref, rs_ref, here)


def attention_kernel(peers, near, near_rs, far, farcore, keys, cot, gain_ref, gk_ref, give_ref, keep_ref, gterm_ref, xf, rs,
                     w, macc, gsum, bias0, bias1, gk, gsems):
    part = far.shape[0]
    length, width = xf.shape
    zl = lax.axis_index("zl")
    c = lax.axis_index("core")
    there = pl.multiple_of(2 * part * (1 - zl), 8)
    pair_rows(c, far, farcore, xf, rs, there)
    macc[...] = jnp.zeros_like(macc)
    scale = F32(HEAD_DIM ** (-0.5))
    scale2 = F32(HEAD_DIM ** (-0.5) * math.log2(math.e))
    cut = HEAD_DIM
    tail = length - cut

    def triangle(n):
        rows = lax.broadcasted_iota(jnp.int32, (n, n), 0)
        cols = lax.broadcasted_iota(jnp.int32, (n, n), 1)
        return jnp.where(rows <= cols, F32(0), F32(-jnp.inf))

    bias0[...] = triangle(cut)
    bias1[...] = triangle(tail)

    def softmax(s, d):
        top = jnp.max(s, axis=0, keepdims=True)
        e = jnp.exp2(s * scale2 - top * scale2)
        inv = 1.0 / jnp.sum(e, axis=0, keepdims=True)
        delta = jnp.sum(e * d, axis=0, keepdims=True) * inv
        p = e * inv
        return p.astype(BF), (p * (d - delta)).astype(BF)

    def begin(a):
        sl = columns(a)
        normed = xf[:, sl] * rs[...]
        q = (normed * gain_ref[:, sl]).astype(BF)
        st = lax.dot_general(keys[0, :, sl], q, NT, preferred_element_type=F32)
        dpt = lax.dot_general(q, cot[0, :, sl], NT, preferred_element_type=F32)
        return sl, q, st, dpt

    def middle(sl, q, st, dpt):
        p0, d0 = softmax(st[:cut, :cut] + bias0[...], dpt[:cut, :cut])
        s1 = jnp.concatenate([st[:cut, cut:], st[cut:, cut:] + bias1[...]], axis=0)
        p1, d1 = softmax(s1, dpt[:, cut:])
        none = jnp.zeros((tail, cut), BF)
        pb = jnp.concatenate([jnp.concatenate([p0, none], axis=0), p1], axis=1)
        dst = jnp.concatenate([jnp.concatenate([d0, none], axis=0), d1], axis=1)
        return sl, q, pb, dst

    def end(a, sl, q, pb, dst):
        dv = jnp.dot(pb, cot[0, :, sl], preferred_element_type=F32)
        dk = jnp.dot(dst, q, preferred_element_type=F32)
        dq = lax.dot_general(dst, keys[0, :, sl], TN, preferred_element_type=F32)
        gk[0, :, sl] = (dk * scale).astype(BF)
        dn = dq * scale + dv
        nd = xf[:, sl] * rs[...] * dn
        gain = gain_ref[:, sl]
        gsum[pl.ds(a, 1), :] = jnp.sum(nd, axis=0, keepdims=True)
        w[:, sl] = gain * dn
        return nd * gain

    def send_group(i):
        sl = pl.ds(pl.multiple_of(i * GROUP * HEAD_DIM, GROUP * HEAD_DIM), GROUP * HEAD_DIM)
        return pltpu.make_async_copy(gk.at[0, :, sl], gk_ref.at[0, :, sl], gsems.at[i])

    def heads(i, _):
        first, second, mean = {}, {}, None
        for step in range(GROUP + 2):
            if step < GROUP:
                first[step] = begin(i * GROUP + step)
            if 0 <= step - 1 < GROUP:
                second[step - 1] = middle(*first.pop(step - 1))
            if 0 <= step - 2 < GROUP:
                one = end(i * GROUP + step - 2, *second.pop(step - 2))
                mean = one if mean is None else mean + one
        macc[...] += mean
        send_group(i).start()
        return 0

    lax.fori_loop(0, NH // GROUP, heads, 0)
    for i in range(peers):
        gterm_ref[i] = gsum[...].astype(BF)
    r = rs[...]
    m = jnp.sum(macc[...], axis=-1, keepdims=True) * (1.0 / width)
    macc[...] = r * r * m
    for ci in range(2):

        @pl.when(c == ci)
        def _(ci=ci):
            def finish(a, _):
                sl = columns(a)
                term = rs[...] * w[:, sl] - macc[...] * xf[:, sl]
                for zi in range(2):
                    mine = part * (2 * zi + ci)
                    other = part * (2 * zi + 1 - ci)
                    keep_ref[SLAB * zi : SLAB * zi + part, sl] = term[mine : mine + part]
                    give_ref[SLAB * zi : SLAB * zi + part, sl] = term[other : other + part].astype(BF)
                return 0

            lax.fori_loop(0, width // HEAD_DIM, finish, 0, unroll=2)

    for i in range(NH // GROUP):
        send_group(i).wait()


def spread_kernel(peers, first, wide_ref):
    total = jnp.sum(first[...].astype(F32), axis=0).astype(BF)
    for i in range(peers):
        wide_ref[i] = total


def between_kernel(keep, got, mine_ref, send_ref):
    zl = lax.axis_index("zl")
    here = pl.ds(pl.multiple_of(SLAB * zl, SLAB), SLAB)
    there = pl.ds(pl.multiple_of(SLAB * (1 - zl), SLAB), SLAB)
    mine_ref[...] = keep[here, :] + got[here, :].astype(F32)
    rows = send_ref.shape[0]
    send_ref[...] = (keep[there, :] + got[there, :].astype(F32))[:rows].astype(BF)


def final_kernel(mine, last, second, trunk_ref, gains_ref):
    total = jnp.sum(second[...].astype(F32), axis=0)
    for r in range(total.shape[0]):
        gains_ref[0:1, r * HEAD_DIM : (r + 1) * HEAD_DIM] = total[r : r + 1, :]
    rows = trunk_ref.shape[0]
    trunk_ref[...] = (mine[...][:rows] + last[...].astype(F32)).astype(BF)


def swap(v, bit):
    return lax.ppermute(v, HEAD, [(i, i ^ bit) for i in range(4)])


def call(kernel, outs, args, name, hbm_in=(), hbm_out=(), scratch=(), cost=(0, 0), limit=LIMIT, alias=None):
    vmem = pl.BlockSpec(memory_space=pltpu.VMEM)
    hbm = pl.BlockSpec(memory_space=pltpu.HBM)
    return pl.pallas_call(
        kernel,
        out_shape=outs,
        in_specs=[hbm if i in hbm_in else vmem for i in range(len(args))],
        out_specs=tuple(hbm if i in hbm_out else vmem for i in range(len(outs))),
        scratch_shapes=list(scratch),
        input_output_aliases=alias or {},
        compiler_params=pltpu.CompilerParams(vmem_limit_bytes=limit),
        cost_estimate=pl.CostEstimate(flops=cost[0], bytes_accessed=cost[1], transcendentals=0),
        name=name,
    )(*args)


def on_device(near, rest, trunk, keys, gains, grad_out):
    part, width = trunk.shape
    length = keys.shape[1]
    shape = jax.ShapeDtypeStruct
    far = swap(trunk, 2)
    core = swap(trunk, 1)
    x_own, rs_own = call(
        own_kernel,
        (shape((part, width), F32), shape((part, HEAD_DIM), F32)),
        (trunk, keys, grad_out, gains),
        "own_rows",
        cost=(0, 8 << 20),
        limit=24 * 1024 * 1024,
    )
    far, x_own = lax.optimization_barrier((far, x_own))
    farcore = swap(far, 1)
    x_near, rs_near = call(
        near_kernel,
        (shape((length, width), F32), shape((length, HEAD_DIM), F32)),
        (x_own, core),
        "near_rows",
    )
    grad_keys, give, keep, gterm, _, _ = call(
        functools.partial(attention_kernel, near),
        (
            shape((1, length, width), BF),
            shape((2 * SLAB, width), BF),
            shape((2 * SLAB, width), F32),
            shape((near, NH, HEAD_DIM), BF),
            shape((length, width), F32),
            shape((length, HEAD_DIM), F32),
        ),
        (x_near, rs_near, far, farcore, keys, grad_out, gains),
        "attention_backward",
        hbm_out=(0,),
        alias={0: 4, 1: 5},
        scratch=[
            pltpu.VMEM((length, width), F32),
            pltpu.VMEM((length, HEAD_DIM), F32),
            pltpu.VMEM((NH, HEAD_DIM), F32),
            pltpu.VMEM((HEAD_DIM, HEAD_DIM), F32),
            pltpu.VMEM((length - HEAD_DIM, length - HEAD_DIM), F32),
            pltpu.VMEM((1, length, width), BF),
            pltpu.SemaphoreType.DMA((NH // GROUP,)),
        ],
        cost=(10 * length * length * width, 16 << 20),
    )
    got = swap(give, 1)
    first = lax.all_to_all(gterm, "y", 0, 0, tiled=True)
    got, first = lax.optimization_barrier((got, first))
    mine, send = call(
        between_kernel, (shape((SLAB, width), F32), shape((part, width), BF)), (keep, got), "add_core"
    )
    send, first = lax.optimization_barrier((send, first))
    last = swap(send, 2)
    (wide,) = call(
        functools.partial(spread_kernel, rest),
        (shape((rest, NH, HEAD_DIM), BF),),
        (first,),
        "sum_near",
        cost=(8 << 30, 0),
    )
    second = lax.all_to_all(wide, ("zh", "x"), 0, 0, tiled=True)
    grad_trunk, grad_gains = call(
        final_kernel, (shape((part, width), BF), shape((1, width), F32)), (mine, last, second), "add_far"
    )
    return grad_trunk, grad_keys, grad_gains


def solution(mesh):
    dp = mesh.shape["dp"]
    near = min(dp, 4)
    zh = 4 if dp >= 16 else 1
    y = dp // near // zh
    fine = Mesh(mesh.devices.reshape(y, zh, near, 2, 2), ("y", "zh", "x", "zl", "core"))
    dps = ("y", "zh", "x")
    return jax.shard_map(
        functools.partial(on_device, y, zh * near),
        mesh=fine,
        in_specs=(
            P(dps + HEAD, None),
            P(HEAD, dps, None),
            P(HEAD, None),
            P(HEAD, dps, None),
        ),
        out_specs=(P(dps + HEAD, None), P(HEAD, dps, None), P(HEAD, None)),
        check_vma=False,
    )
```

```python
import functools
import math

import jax
import jax.numpy as jnp
from jax import lax
from jax.experimental import pallas as pl
from jax.experimental.pallas import tpu as pltpu
from jax.sharding import Mesh
from jax.sharding import PartitionSpec as P

NH = 32
HEAD_DIM = 128
SENT = 8
SLAB = 48
BF = jnp.bfloat16
F32 = jnp.float32
NT = (((1,), (1,)), ((), ()))
TN = (((0,), (0,)), ((), ()))
HEAD = ("zl", "core")
LIMIT = 24 * 1024 * 1024


def columns(a):
    if isinstance(a, int):
        return pl.ds(a * HEAD_DIM, HEAD_DIM)
    return pl.ds(pl.multiple_of(a * HEAD_DIM, HEAD_DIM), HEAD_DIM)


def pair_rows(c, first, second, x_ref, rs_ref, base):
    part, width = first.shape
    for ci in range(2):

        @pl.when(c == ci)
        def _(ci=ci):
            low, high = (first, second) if ci == 0 else (second, first)

            def put(a, acc):
                sl = columns(a)
                v = jnp.concatenate([low[:, sl].astype(F32), high[:, sl].astype(F32)], axis=0)
                x_ref[pl.ds(base, 2 * part), sl] = v
                return acc + v * v

            total = lax.fori_loop(0, width // HEAD_DIM, put, jnp.zeros((2 * part, HEAD_DIM), F32), unroll=4)
            mean = jnp.sum(total, axis=-1, keepdims=True) * (1.0 / width)
            rs_ref[pl.ds(base, 2 * part), :] = jnp.broadcast_to(lax.rsqrt(mean + 1e-05), (2 * part, HEAD_DIM))


def own_kernel(own, keys, cot, gain, x_ref, rs_ref):
    part, width = own.shape

    def put(a, acc):
        sl = columns(a)
        v = own[:, sl].astype(F32)
        x_ref[:, sl] = v
        return acc + v * v

    total = lax.fori_loop(0, width // HEAD_DIM, put, jnp.zeros((part, HEAD_DIM), F32), unroll=4)
    mean = jnp.sum(total, axis=-1, keepdims=True) * (1.0 / width)
    rs_ref[...] = jnp.broadcast_to(lax.rsqrt(mean + 1e-05), (part, HEAD_DIM))


def far_rows(zl, c, ref, x_ref, rs_ref, same):
    part, width = ref.shape
    for p in range(4):

        @pl.when((zl == 1 - p // 2) & (c == (p % 2 if same else 1 - p % 2)))
        def _(p=p):
            def put(a, acc):
                sl = columns(a)
                v = ref[:, sl].astype(F32)
                x_ref[part * p : part * (p + 1), sl] = v
                return acc + v * v

            total = lax.fori_loop(0, width // HEAD_DIM, put, jnp.zeros((part, HEAD_DIM), F32), unroll=4)
            mean = jnp.sum(total, axis=-1, keepdims=True) * (1.0 / width)
            rs_ref[part * p : part * (p + 1), :] = jnp.broadcast_to(lax.rsqrt(mean + 1e-05), (part, HEAD_DIM))


def near_kernel(own, core, far, x_ref, rs_ref):
    zl = lax.axis_index("zl")
    c = lax.axis_index("core")
    here = pl.multiple_of(2 * own.shape[0] * zl, 8)
    pair_rows(c, own, core, x_ref, rs_ref, here)
    far_rows(zl, c, far, x_ref, rs_ref, True)


def attention_kernel(peers, near, near_rs, farcore, keys, cot, gain_ref, gk_ref, give_ref, keep_ref, gterm_ref, xf, rs,
                     w, macc, gsum, bias0, bias1, gk, gsems):
    part = farcore.shape[0]
    length, width = xf.shape
    zl = lax.axis_index("zl")
    c = lax.axis_index("core")
    far_rows(zl, c, farcore, xf, rs, False)
    macc[...] = jnp.zeros_like(macc)
    scale = F32(HEAD_DIM ** (-0.5))
    scale2 = F32(HEAD_DIM ** (-0.5) * math.log2(math.e))
    cut = HEAD_DIM
    tail = length - cut

    def triangle(n):
        rows = lax.broadcasted_iota(jnp.int32, (n, n), 0)
        cols = lax.broadcasted_iota(jnp.int32, (n, n), 1)
        return jnp.where(rows <= cols, F32(0), F32(-jnp.inf))

    bias0[...] = triangle(cut)
    bias1[...] = triangle(tail)

    def softmax(s, d):
        top = jnp.max(s, axis=0, keepdims=True)
        e = jnp.exp2(s * scale2 - top * scale2)
        inv = 1.0 / jnp.sum(e, axis=0, keepdims=True)
        delta = jnp.sum(e * d, axis=0, keepdims=True) * inv
        p = e * inv
        return p.astype(BF), (p * (d - delta)).astype(BF)

    def begin(a):
        sl = columns(a)
        normed = xf[:, sl] * rs[...]
        q = (normed * gain_ref[:, sl]).astype(BF)
        st = lax.dot_general(keys[0, :, sl], q, NT, preferred_element_type=F32)
        dpt = lax.dot_general(q, cot[0, :, sl], NT, preferred_element_type=F32)
        return sl, q, st, dpt

    def middle(sl, q, st, dpt):
        p0, d0 = softmax(st[:cut, :cut] + bias0[...], dpt[:cut, :cut])
        s1 = jnp.concatenate([st[:cut, cut:], st[cut:, cut:] + bias1[...]], axis=0)
        p1, d1 = softmax(s1, dpt[:, cut:])
        none = jnp.zeros((tail, cut), BF)
        pb = jnp.concatenate([jnp.concatenate([p0, none], axis=0), p1], axis=1)
        dst = jnp.concatenate([jnp.concatenate([d0, none], axis=0), d1], axis=1)
        return sl, q, pb, dst

    def end(a, sl, q, pb, dst):
        dv = jnp.dot(pb, cot[0, :, sl], preferred_element_type=F32)
        dk = jnp.dot(dst, q, preferred_element_type=F32)
        dq = lax.dot_general(dst, keys[0, :, sl], TN, preferred_element_type=F32)
        gk[0, :, sl] = (dk * scale).astype(BF)
        dn = dq * scale + dv
        nd = xf[:, sl] * rs[...] * dn
        gain = gain_ref[:, sl]
        gsum[pl.ds(a, 1), :] = jnp.sum(nd, axis=0, keepdims=True)
        w[:, sl] = gain * dn
        return nd * gain

    def send_group(i):
        sl = pl.ds(i * SENT * HEAD_DIM, SENT * HEAD_DIM)
        return pltpu.make_async_copy(gk.at[0, :, sl], gk_ref.at[0, :, sl], gsems.at[i])

    first, second, mean = {}, {}, None
    for step in range(NH + 2):
        if step < NH:
            first[step] = begin(step)
        if 0 <= step - 1 < NH:
            second[step - 1] = middle(*first.pop(step - 1))
        if 0 <= step - 2 < NH:
            one = end(step - 2, *second.pop(step - 2))
            mean = one if mean is None else mean + one
            if (step - 1) % SENT == 0:
                send_group((step - 1) // SENT - 1).start()
            if (step - 1) % 8 == 0:
                macc[...] += mean
                mean = None
    for i in range(peers):
        gterm_ref[i] = gsum[...].astype(BF)
    r = rs[...]
    m = jnp.sum(macc[...], axis=-1, keepdims=True) * (1.0 / width)
    macc[...] = r * r * m
    for ci in range(2):

        @pl.when(c == ci)
        def _(ci=ci):
            def finish(a, _):
                sl = columns(a)
                term = rs[...] * w[:, sl] - macc[...] * xf[:, sl]
                for zi in range(2):
                    mine = part * (2 * zi + ci)
                    other = part * (2 * zi + 1 - ci)
                    keep_ref[SLAB * zi : SLAB * zi + part, sl] = term[mine : mine + part]
                    give_ref[SLAB * zi : SLAB * zi + part, sl] = term[other : other + part].astype(BF)
                return 0

            lax.fori_loop(0, width // HEAD_DIM, finish, 0, unroll=2)

    for i in range(NH // SENT):
        send_group(i).wait()


def spread_kernel(peers, first, wide_ref):
    total = jnp.sum(first[...].astype(F32), axis=0).astype(BF)
    for i in range(peers):
        wide_ref[i] = total


def between_kernel(keep, got, mine_ref, send_ref):
    zl = lax.axis_index("zl")
    here = pl.ds(pl.multiple_of(SLAB * zl, SLAB), SLAB)
    there = pl.ds(pl.multiple_of(SLAB * (1 - zl), SLAB), SLAB)
    mine_ref[...] = keep[here, :] + got[here, :].astype(F32)
    rows = send_ref.shape[0]
    send_ref[...] = (keep[there, :] + got[there, :].astype(F32))[:rows].astype(BF)


def final_kernel(mine, last, second, trunk_ref, gains_ref):
    total = jnp.sum(second[...].astype(F32), axis=0)
    for r in range(total.shape[0]):
        gains_ref[0:1, r * HEAD_DIM : (r + 1) * HEAD_DIM] = total[r : r + 1, :]
    rows = trunk_ref.shape[0]
    trunk_ref[...] = (mine[...][:rows] + last[...].astype(F32)).astype(BF)


def swap(v, bit):
    return lax.ppermute(v, HEAD, [(i, i ^ bit) for i in range(4)])


def call(kernel, outs, args, name, hbm_in=(), hbm_out=(), scratch=(), cost=(0, 0), limit=LIMIT, alias=None):
    vmem = pl.BlockSpec(memory_space=pltpu.VMEM)
    hbm = pl.BlockSpec(memory_space=pltpu.HBM)
    return pl.pallas_call(
        kernel,
        out_shape=outs,
        in_specs=[hbm if i in hbm_in else vmem for i in range(len(args))],
        out_specs=tuple(hbm if i in hbm_out else vmem for i in range(len(outs))),
        scratch_shapes=list(scratch),
        input_output_aliases=alias or {},
        compiler_params=pltpu.CompilerParams(vmem_limit_bytes=limit),
        cost_estimate=pl.CostEstimate(flops=cost[0], bytes_accessed=cost[1], transcendentals=0),
        name=name,
    )(*args)


def on_device(near, rest, trunk, keys, gains, grad_out):
    part, width = trunk.shape
    length = keys.shape[1]
    shape = jax.ShapeDtypeStruct
    far = swap(trunk, 2)
    core = swap(trunk, 1)
    x_own, rs_own = call(
        own_kernel,
        (shape((part, width), F32), shape((part, HEAD_DIM), F32)),
        (trunk, keys, grad_out, gains),
        "own_rows",
        cost=(0, 8 << 20),
        limit=24 * 1024 * 1024,
    )
    far, x_own = lax.optimization_barrier((far, x_own))
    farcore = swap(far, 1)
    x_near, rs_near = call(
        near_kernel,
        (shape((length, width), F32), shape((length, HEAD_DIM), F32)),
        (x_own, core, far),
        "near_rows",
    )
    grad_keys, give, keep, gterm, _, _ = call(
        functools.partial(attention_kernel, near),
        (
            shape((1, length, width), BF),
            shape((2 * SLAB, width), BF),
            shape((2 * SLAB, width), F32),
            shape((near, NH, HEAD_DIM), BF),
            shape((length, width), F32),
            shape((length, HEAD_DIM), F32),
        ),
        (x_near, rs_near, farcore, keys, grad_out, gains),
        "attention_backward",
        hbm_out=(0,),
        alias={0: 4, 1: 5},
        scratch=[
            pltpu.VMEM((length, width), F32),
            pltpu.VMEM((length, HEAD_DIM), F32),
            pltpu.VMEM((NH, HEAD_DIM), F32),
            pltpu.VMEM((HEAD_DIM, HEAD_DIM), F32),
            pltpu.VMEM((length - HEAD_DIM, length - HEAD_DIM), F32),
            pltpu.VMEM((1, length, width), BF),
            pltpu.SemaphoreType.DMA((NH // SENT,)),
        ],
        cost=(10 * length * length * width, 16 << 20),
    )
    got = swap(give, 1)
    first = lax.all_to_all(gterm, "y", 0, 0, tiled=True)
    got, first = lax.optimization_barrier((got, first))
    mine, send = call(
        between_kernel, (shape((SLAB, width), F32), shape((part, width), BF)), (keep, got), "add_core"
    )
    send, first = lax.optimization_barrier((send, first))
    last = swap(send, 2)
    (wide,) = call(
        functools.partial(spread_kernel, rest),
        (shape((rest, NH, HEAD_DIM), BF),),
        (first,),
        "sum_near",
        cost=(8 << 30, 0),
    )
    second = lax.all_to_all(wide, ("zh", "x"), 0, 0, tiled=True)
    grad_trunk, grad_gains = call(
        final_kernel, (shape((part, width), BF), shape((1, width), F32)), (mine, last, second), "add_far"
    )
    return grad_trunk, grad_keys, grad_gains


def solution(mesh):
    dp = mesh.shape["dp"]
    near = min(dp, 4)
    zh = 4 if dp >= 16 else 1
    y = dp // near // zh
    fine = Mesh(mesh.devices.reshape(y, zh, near, 2, 2), ("y", "zh", "x", "zl", "core"))
    dps = ("y", "zh", "x")
    return jax.shard_map(
        functools.partial(on_device, y, zh * near),
        mesh=fine,
        in_specs=(
            P(dps + HEAD, None),
            P(HEAD, dps, None),
            P(HEAD, None),
            P(HEAD, dps, None),
        ),
        out_specs=(P(dps + HEAD, None), P(HEAD, dps, None), P(HEAD, None)),
        check_vma=False,
    )
```

```python
import functools
import math

import jax
import jax.numpy as jnp
from jax import lax
from jax.experimental import pallas as pl
from jax.experimental.pallas import tpu as pltpu
from jax.sharding import Mesh
from jax.sharding import PartitionSpec as P

NH = 32
HEAD_DIM = 128
SENT = 8
SLAB = 48
BF = jnp.bfloat16
F32 = jnp.float32
NT = (((1,), (1,)), ((), ()))
TN = (((0,), (0,)), ((), ()))
HEAD = ("zl", "core")
LIMIT = 24 * 1024 * 1024


def columns(a):
    if isinstance(a, int):
        return pl.ds(a * HEAD_DIM, HEAD_DIM)
    return pl.ds(pl.multiple_of(a * HEAD_DIM, HEAD_DIM), HEAD_DIM)


def pair_rows(c, first, second, x_ref, rs_ref, base):
    part, width = first.shape
    for ci in range(2):

        @pl.when(c == ci)
        def _(ci=ci):
            low, high = (first, second) if ci == 0 else (second, first)

            def put(a, acc):
                sl = columns(a)
                v = jnp.concatenate([low[:, sl].astype(F32), high[:, sl].astype(F32)], axis=0)
                x_ref[pl.ds(base, 2 * part), sl] = v
                return acc + v * v

            total = lax.fori_loop(0, width // HEAD_DIM, put, jnp.zeros((2 * part, HEAD_DIM), F32), unroll=4)
            mean = jnp.sum(total, axis=-1, keepdims=True) * (1.0 / width)
            rs_ref[pl.ds(base, 2 * part), :] = jnp.broadcast_to(lax.rsqrt(mean + 1e-05), (2 * part, HEAD_DIM))


def own_kernel(own, keys, cot, gain, x_ref, rs_ref):
    part, width = own.shape

    def put(a, acc):
        sl = columns(a)
        v = own[:, sl].astype(F32)
        x_ref[:, sl] = v
        return acc + v * v

    total = lax.fori_loop(0, width // HEAD_DIM, put, jnp.zeros((part, HEAD_DIM), F32), unroll=4)
    mean = jnp.sum(total, axis=-1, keepdims=True) * (1.0 / width)
    rs_ref[...] = jnp.broadcast_to(lax.rsqrt(mean + 1e-05), (part, HEAD_DIM))


def far_rows(zl, c, ref, x_ref, rs_ref, same):
    part, width = ref.shape
    for p in range(4):

        @pl.when((zl == 1 - p // 2) & (c == (p % 2 if same else 1 - p % 2)))
        def _(p=p):
            def put(a, acc):
                sl = columns(a)
                v = ref[:, sl].astype(F32)
                x_ref[part * p : part * (p + 1), sl] = v
                return acc + v * v

            total = lax.fori_loop(0, width // HEAD_DIM, put, jnp.zeros((part, HEAD_DIM), F32), unroll=4)
            mean = jnp.sum(total, axis=-1, keepdims=True) * (1.0 / width)
            rs_ref[part * p : part * (p + 1), :] = jnp.broadcast_to(lax.rsqrt(mean + 1e-05), (part, HEAD_DIM))


def near_kernel(own, core, far, x_ref, rs_ref):
    zl = lax.axis_index("zl")
    c = lax.axis_index("core")
    here = pl.multiple_of(2 * own.shape[0] * zl, 8)
    pair_rows(c, own, core, x_ref, rs_ref, here)
    far_rows(zl, c, far, x_ref, rs_ref, True)


def attention_kernel(peers, near, near_rs, farcore, keys, cot, gain_ref, gk_ref, give_ref, keep_ref, gterm_ref, xf, rs,
                     w, macc, gsum, bias0, bias1, gk, gsems):
    part = farcore.shape[0]
    length, width = xf.shape
    zl = lax.axis_index("zl")
    c = lax.axis_index("core")
    far_rows(zl, c, farcore, xf, rs, False)
    macc[...] = jnp.zeros_like(macc)
    scale = F32(HEAD_DIM ** (-0.5))
    scale2 = F32(HEAD_DIM ** (-0.5) * math.log2(math.e))
    cut = HEAD_DIM
    tail = length - cut

    def triangle(n):
        rows = lax.broadcasted_iota(jnp.int32, (n, n), 0)
        cols = lax.broadcasted_iota(jnp.int32, (n, n), 1)
        return jnp.where(rows <= cols, F32(0), F32(-jnp.inf))

    bias0[...] = triangle(cut)
    bias1[...] = triangle(tail)

    def softmax(s, d):
        top = jnp.max(s, axis=0, keepdims=True)
        e = jnp.exp2(s * scale2 - top * scale2)
        inv = 1.0 / jnp.sum(e, axis=0, keepdims=True)
        delta = jnp.sum(e * d, axis=0, keepdims=True) * inv
        p = e * inv
        return p.astype(BF), (p * (d - delta)).astype(BF)

    def begin(a):
        sl = columns(a)
        normed = xf[:, sl] * rs[...]
        q = (normed * gain_ref[:, sl]).astype(BF)
        st = lax.dot_general(keys[0, :, sl], q, NT, preferred_element_type=F32)
        dpt = lax.dot_general(q, cot[0, :, sl], NT, preferred_element_type=F32)
        return sl, q, st, dpt

    def middle(sl, q, st, dpt):
        p0, d0 = softmax(st[:cut, :cut] + bias0[...], dpt[:cut, :cut])
        s1 = jnp.concatenate([st[:cut, cut:], st[cut:, cut:] + bias1[...]], axis=0)
        p1, d1 = softmax(s1, dpt[:, cut:])
        none = jnp.zeros((tail, cut), BF)
        pb = jnp.concatenate([jnp.concatenate([p0, none], axis=0), p1], axis=1)
        dst = jnp.concatenate([jnp.concatenate([d0, none], axis=0), d1], axis=1)
        return sl, q, pb, dst

    def end(a, sl, q, pb, dst):
        dv = jnp.dot(pb, cot[0, :, sl], preferred_element_type=F32)
        dk = jnp.dot(dst, q, preferred_element_type=F32)
        dq = lax.dot_general(dst, keys[0, :, sl], TN, preferred_element_type=F32)
        gk[0, :, sl] = (dk * scale).astype(BF)
        dn = dq * scale + dv
        nd = xf[:, sl] * rs[...] * dn
        gain = gain_ref[:, sl]
        gsum[pl.ds(a, 1), :] = jnp.sum(nd, axis=0, keepdims=True)
        w[:, sl] = gain * dn
        return nd * gain

    def send_group(i):
        sl = pl.ds(i * SENT * HEAD_DIM, SENT * HEAD_DIM)
        return pltpu.make_async_copy(gk.at[0, :, sl], gk_ref.at[0, :, sl], gsems.at[i])

    first, second, mean = {}, {}, None
    for step in range(NH + 2):
        if step < NH:
            first[step] = begin(step)
        if 0 <= step - 1 < NH:
            second[step - 1] = middle(*first.pop(step - 1))
        if 0 <= step - 2 < NH:
            one = end(step - 2, *second.pop(step - 2))
            mean = one if mean is None else mean + one
            if (step - 1) % SENT == 0:
                send_group((step - 1) // SENT - 1).start()
            if (step - 1) % 8 == 0:
                macc[...] += mean
                mean = None
    for i in range(peers):
        gterm_ref[i] = gsum[...].astype(BF)
    r = rs[...]
    m = jnp.sum(macc[...], axis=-1, keepdims=True) * (1.0 / width)
    macc[...] = r * r * m
    for ci in range(2):

        @pl.when(c == ci)
        def _(ci=ci):
            def finish(a, _):
                sl = columns(a)
                term = rs[...] * w[:, sl] - macc[...] * xf[:, sl]
                for zi in range(2):
                    mine = part * (2 * zi + ci)
                    other = part * (2 * zi + 1 - ci)
                    keep_ref[SLAB * zi : SLAB * zi + part, sl] = term[mine : mine + part]
                    give_ref[SLAB * zi : SLAB * zi + part, sl] = term[other : other + part].astype(BF)
                return 0

            lax.fori_loop(0, width // HEAD_DIM, finish, 0, unroll=2)

    for i in range(NH // SENT):
        send_group(i).wait()


def spread_kernel(peers, first, wide_ref):
    total = jnp.sum(first[...].astype(F32), axis=0).astype(BF)
    for i in range(peers):
        wide_ref[i] = total


def between_kernel(keep, got, mine_ref, send_ref):
    zl = lax.axis_index("zl")
    here = pl.ds(pl.multiple_of(SLAB * zl, SLAB), SLAB)
    there = pl.ds(pl.multiple_of(SLAB * (1 - zl), SLAB), SLAB)
    mine_ref[...] = keep[here, :] + got[here, :].astype(F32)
    rows = send_ref.shape[0]
    send_ref[...] = (keep[there, :] + got[there, :].astype(F32))[:rows].astype(BF)


def final_kernel(mine, last, second, trunk_ref, gains_ref):
    total = jnp.sum(second[...].astype(F32), axis=0)
    for r in range(total.shape[0]):
        gains_ref[0:1, r * HEAD_DIM : (r + 1) * HEAD_DIM] = total[r : r + 1, :]
    rows = trunk_ref.shape[0]
    trunk_ref[...] = (mine[...][:rows] + last[...].astype(F32)).astype(BF)


def swap(v, bit):
    return lax.ppermute(v, HEAD, [(i, i ^ bit) for i in range(4)])


def call(kernel, outs, args, name, hbm_in=(), hbm_out=(), scratch=(), cost=(0, 0), limit=LIMIT, alias=None):
    vmem = pl.BlockSpec(memory_space=pltpu.VMEM)
    hbm = pl.BlockSpec(memory_space=pltpu.HBM)
    return pl.pallas_call(
        kernel,
        out_shape=outs,
        in_specs=[hbm if i in hbm_in else vmem for i in range(len(args))],
        out_specs=tuple(hbm if i in hbm_out else vmem for i in range(len(outs))),
        scratch_shapes=list(scratch),
        input_output_aliases=alias or {},
        compiler_params=pltpu.CompilerParams(vmem_limit_bytes=limit),
        cost_estimate=pl.CostEstimate(flops=cost[0], bytes_accessed=cost[1], transcendentals=0),
        name=name,
    )(*args)


def on_device(near, rest, trunk, keys, gains, grad_out):
    part, width = trunk.shape
    length = keys.shape[1]
    shape = jax.ShapeDtypeStruct
    far = swap(trunk, 2)
    core = swap(trunk, 1)
    x_own, rs_own = call(
        own_kernel,
        (shape((part, width), F32), shape((part, HEAD_DIM), F32)),
        (trunk, keys, grad_out, gains),
        "own_rows",
        cost=(0, 8 << 20),
        limit=24 * 1024 * 1024,
    )
    far, x_own = lax.optimization_barrier((far, x_own))
    farcore = swap(far, 1)
    x_near, rs_near = call(
        near_kernel,
        (shape((length, width), F32), shape((length, HEAD_DIM), F32)),
        (x_own, core, far),
        "near_rows",
    )
    grad_keys, give, keep, gterm, _, _ = call(
        functools.partial(attention_kernel, near),
        (
            shape((1, length, width), BF),
            shape((2 * SLAB, width), BF),
            shape((2 * SLAB, width), F32),
            shape((near, NH, HEAD_DIM), BF),
            shape((length, width), F32),
            shape((length, HEAD_DIM), F32),
        ),
        (x_near, rs_near, farcore, keys, grad_out, gains),
        "attention_backward",
        hbm_out=(0,),
        alias={0: 4, 1: 5},
        scratch=[
            pltpu.VMEM((length, width), F32),
            pltpu.VMEM((length, HEAD_DIM), F32),
            pltpu.VMEM((NH, HEAD_DIM), F32),
            pltpu.VMEM((HEAD_DIM, HEAD_DIM), F32),
            pltpu.VMEM((length - HEAD_DIM, length - HEAD_DIM), F32),
            pltpu.VMEM((1, length, width), BF),
            pltpu.SemaphoreType.DMA((NH // SENT,)),
        ],
        cost=(10 * length * length * width, 16 << 20),
    )
    got = swap(give, 1)
    mine, send = call(
        between_kernel, (shape((SLAB, width), F32), shape((part, width), BF)), (keep, got), "add_core", cost=(0, 0)
    )
    last = swap(send, 2)
    first = lax.all_to_all(gterm, "y", 0, 0, tiled=True)
    (wide,) = call(
        functools.partial(spread_kernel, rest),
        (shape((rest, NH, HEAD_DIM), BF),),
        (first,),
        "sum_near",
        cost=(8 << 30, 0),
    )
    second = lax.all_to_all(wide, ("zh", "x"), 0, 0, tiled=True)
    grad_trunk, grad_gains = call(
        final_kernel, (shape((part, width), BF), shape((1, width), F32)), (mine, last, second), "add_far"
    )
    return grad_trunk, grad_keys, grad_gains


def solution(mesh):
    dp = mesh.shape["dp"]
    near = min(dp, 4)
    zh = 4 if dp >= 16 else 1
    y = dp // near // zh
    fine = Mesh(mesh.devices.reshape(y, zh, near, 2, 2), ("y", "zh", "x", "zl", "core"))
    dps = ("y", "zh", "x")
    return jax.shard_map(
        functools.partial(on_device, y, zh * near),
        mesh=fine,
        in_specs=(
            P(dps + HEAD, None),
            P(HEAD, dps, None),
            P(HEAD, None),
            P(HEAD, dps, None),
        ),
        out_specs=(P(dps + HEAD, None), P(HEAD, dps, None), P(HEAD, None)),
        check_vma=False,
    )
```

```python
import functools
import math

import jax
import jax.numpy as jnp
from jax import lax
from jax.experimental import pallas as pl
from jax.experimental.pallas import tpu as pltpu
from jax.sharding import Mesh
from jax.sharding import PartitionSpec as P

NH = 32
HEAD_DIM = 128
SENT = 8
SLAB = 48
BF = jnp.bfloat16
F32 = jnp.float32
NT = (((1,), (1,)), ((), ()))
TN = (((0,), (0,)), ((), ()))
HEAD = ("zl", "core")
LIMIT = 24 * 1024 * 1024


def columns(a):
    if isinstance(a, int):
        return pl.ds(a * HEAD_DIM, HEAD_DIM)
    return pl.ds(pl.multiple_of(a * HEAD_DIM, HEAD_DIM), HEAD_DIM)


def pair_rows(c, first, second, x_ref, rs_ref, base):
    part, width = first.shape
    for ci in range(2):

        @pl.when(c == ci)
        def _(ci=ci):
            low, high = (first, second) if ci == 0 else (second, first)

            def put(a, acc):
                sl = columns(a)
                v = jnp.concatenate([low[:, sl].astype(F32), high[:, sl].astype(F32)], axis=0)
                x_ref[pl.ds(base, 2 * part), sl] = v
                return acc + v * v

            total = lax.fori_loop(0, width // HEAD_DIM, put, jnp.zeros((2 * part, HEAD_DIM), F32), unroll=4)
            mean = jnp.sum(total, axis=-1, keepdims=True) * (1.0 / width)
            rs_ref[pl.ds(base, 2 * part), :] = jnp.broadcast_to(lax.rsqrt(mean + 1e-05), (2 * part, HEAD_DIM))


def own_kernel(own, keys, cot, gain, x_ref, rs_ref):
    part, width = own.shape

    def put(a, acc):
        sl = columns(a)
        v = own[:, sl].astype(F32)
        x_ref[:, sl] = v
        return acc + v * v

    total = lax.fori_loop(0, width // HEAD_DIM, put, jnp.zeros((part, HEAD_DIM), F32), unroll=4)
    mean = jnp.sum(total, axis=-1, keepdims=True) * (1.0 / width)
    rs_ref[...] = jnp.broadcast_to(lax.rsqrt(mean + 1e-05), (part, HEAD_DIM))


def far_rows(zl, c, ref, x_ref, rs_ref, same):
    part, width = ref.shape
    for p in range(4):

        @pl.when((zl == 1 - p // 2) & (c == (p % 2 if same else 1 - p % 2)))
        def _(p=p):
            def put(a, acc):
                sl = columns(a)
                v = ref[:, sl].astype(F32)
                x_ref[part * p : part * (p + 1), sl] = v
                return acc + v * v

            total = lax.fori_loop(0, width // HEAD_DIM, put, jnp.zeros((part, HEAD_DIM), F32), unroll=4)
            mean = jnp.sum(total, axis=-1, keepdims=True) * (1.0 / width)
            rs_ref[part * p : part * (p + 1), :] = jnp.broadcast_to(lax.rsqrt(mean + 1e-05), (part, HEAD_DIM))


def near_kernel(own, core, far, x_ref, rs_ref):
    zl = lax.axis_index("zl")
    c = lax.axis_index("core")
    here = pl.multiple_of(2 * own.shape[0] * zl, 8)
    pair_rows(c, own, core, x_ref, rs_ref, here)
    far_rows(zl, c, far, x_ref, rs_ref, True)


def attention_kernel(peers, near, near_rs, farcore, keys, cot, gain_ref, gk_ref, give_ref, keep_ref, gterm_hbm, xf, rs,
                     gterm_ref, gterm_sem, w, macc, gsum, bias0, bias1, gk, gsems):
    part = farcore.shape[0]
    length, width = xf.shape
    zl = lax.axis_index("zl")
    c = lax.axis_index("core")
    far_rows(zl, c, farcore, xf, rs, False)
    macc[...] = jnp.zeros_like(macc)
    scale = F32(HEAD_DIM ** (-0.5))
    scale2 = F32(HEAD_DIM ** (-0.5) * math.log2(math.e))
    cut = HEAD_DIM
    tail = length - cut

    def triangle(n):
        rows = lax.broadcasted_iota(jnp.int32, (n, n), 0)
        cols = lax.broadcasted_iota(jnp.int32, (n, n), 1)
        return jnp.where(rows <= cols, F32(0), F32(-jnp.inf))

    bias0[...] = triangle(cut)
    bias1[...] = triangle(tail)

    def softmax(s, d):
        top = jnp.max(s, axis=0, keepdims=True)
        e = jnp.exp2(s * scale2 - top * scale2)
        inv = 1.0 / jnp.sum(e, axis=0, keepdims=True)
        delta = jnp.sum(e * d, axis=0, keepdims=True) * inv
        p = e * inv
        return p.astype(BF), (p * (d - delta)).astype(BF)

    def begin(a):
        sl = columns(a)
        normed = xf[:, sl] * rs[...]
        q = (normed * gain_ref[:, sl]).astype(BF)
        st = lax.dot_general(keys[0, :, sl], q, NT, preferred_element_type=F32)
        dpt = lax.dot_general(q, cot[0, :, sl], NT, preferred_element_type=F32)
        return sl, q, st, dpt

    def middle(sl, q, st, dpt):
        p0, d0 = softmax(st[:cut, :cut] + bias0[...], dpt[:cut, :cut])
        s1 = jnp.concatenate([st[:cut, cut:], st[cut:, cut:] + bias1[...]], axis=0)
        p1, d1 = softmax(s1, dpt[:, cut:])
        none = jnp.zeros((tail, cut), BF)
        pb = jnp.concatenate([jnp.concatenate([p0, none], axis=0), p1], axis=1)
        dst = jnp.concatenate([jnp.concatenate([d0, none], axis=0), d1], axis=1)
        return sl, q, pb, dst

    def end(a, sl, q, pb, dst):
        dv = jnp.dot(pb, cot[0, :, sl], preferred_element_type=F32)
        dk = jnp.dot(dst, q, preferred_element_type=F32)
        dq = lax.dot_general(dst, keys[0, :, sl], TN, preferred_element_type=F32)
        gk[0, :, sl] = (dk * scale).astype(BF)
        dn = dq * scale + dv
        nd = xf[:, sl] * rs[...] * dn
        gain = gain_ref[:, sl]
        gsum[pl.ds(a, 1), :] = jnp.sum(nd, axis=0, keepdims=True)
        w[:, sl] = gain * dn
        return nd * gain

    def send_group(i):
        sl = pl.ds(i * SENT * HEAD_DIM, SENT * HEAD_DIM)
        return pltpu.make_async_copy(gk.at[0, :, sl], gk_ref.at[0, :, sl], gsems.at[i])

    first, second, mean = {}, {}, None
    for step in range(NH + 2):
        if step < NH:
            first[step] = begin(step)
        if 0 <= step - 1 < NH:
            second[step - 1] = middle(*first.pop(step - 1))
        if 0 <= step - 2 < NH:
            one = end(step - 2, *second.pop(step - 2))
            mean = one if mean is None else mean + one
            if (step - 1) % SENT == 0:
                send_group((step - 1) // SENT - 1).start()
            if (step - 1) % 8 == 0:
                macc[...] += mean
                mean = None
    for i in range(peers):
        gterm_ref[i] = gsum[...].astype(BF)
    send_gterm = pltpu.make_async_copy(gterm_ref, gterm_hbm, gterm_sem.at[0])
    send_gterm.start()
    r = rs[...]
    m = jnp.sum(macc[...], axis=-1, keepdims=True) * (1.0 / width)
    macc[...] = r * r * m
    for ci in range(2):

        @pl.when(c == ci)
        def _(ci=ci):
            def finish(a, _):
                sl = columns(a)
                term = rs[...] * w[:, sl] - macc[...] * xf[:, sl]
                for zi in range(2):
                    mine = part * (2 * zi + ci)
                    other = part * (2 * zi + 1 - ci)
                    keep_ref[SLAB * zi : SLAB * zi + part, sl] = term[mine : mine + part]
                    give_ref[SLAB * zi : SLAB * zi + part, sl] = term[other : other + part].astype(BF)
                return 0

            lax.fori_loop(0, width // HEAD_DIM, finish, 0, unroll=2)

    for i in range(NH // SENT):
        send_group(i).wait()
    send_gterm.wait()


def spread_kernel(peers, first, wide_ref):
    total = jnp.sum(first[...].astype(F32), axis=0).astype(BF)
    for i in range(peers):
        wide_ref[i] = total


def between_kernel(keep, got, mine_ref, send_ref):
    zl = lax.axis_index("zl")
    here = pl.ds(pl.multiple_of(SLAB * zl, SLAB), SLAB)
    there = pl.ds(pl.multiple_of(SLAB * (1 - zl), SLAB), SLAB)
    mine_ref[...] = keep[here, :] + got[here, :].astype(F32)
    rows = send_ref.shape[0]
    send_ref[...] = (keep[there, :] + got[there, :].astype(F32))[:rows].astype(BF)


def final_kernel(mine, last, second, trunk_ref, gains_ref):
    total = jnp.sum(second[...].astype(F32), axis=0)
    for r in range(total.shape[0]):
        gains_ref[0:1, r * HEAD_DIM : (r + 1) * HEAD_DIM] = total[r : r + 1, :]
    rows = trunk_ref.shape[0]
    trunk_ref[...] = (mine[...][:rows] + last[...].astype(F32)).astype(BF)


def swap(v, bit):
    return lax.ppermute(v, HEAD, [(i, i ^ bit) for i in range(4)])


def call(kernel, outs, args, name, hbm_in=(), hbm_out=(), scratch=(), cost=(0, 0), limit=LIMIT, alias=None):
    vmem = pl.BlockSpec(memory_space=pltpu.VMEM)
    hbm = pl.BlockSpec(memory_space=pltpu.HBM)
    return pl.pallas_call(
        kernel,
        out_shape=outs,
        in_specs=[hbm if i in hbm_in else vmem for i in range(len(args))],
        out_specs=tuple(hbm if i in hbm_out else vmem for i in range(len(outs))),
        scratch_shapes=list(scratch),
        input_output_aliases=alias or {},
        compiler_params=pltpu.CompilerParams(vmem_limit_bytes=limit),
        cost_estimate=pl.CostEstimate(flops=cost[0], bytes_accessed=cost[1], transcendentals=0),
        name=name,
    )(*args)


def on_device(near, rest, trunk, keys, gains, grad_out):
    part, width = trunk.shape
    length = keys.shape[1]
    shape = jax.ShapeDtypeStruct
    far = swap(trunk, 2)
    core = swap(trunk, 1)
    x_own, rs_own = call(
        own_kernel,
        (shape((part, width), F32), shape((part, HEAD_DIM), F32)),
        (trunk, keys, grad_out, gains),
        "own_rows",
        cost=(0, 8 << 20),
        limit=24 * 1024 * 1024,
    )
    far, x_own = lax.optimization_barrier((far, x_own))
    farcore = swap(far, 1)
    x_near, rs_near = call(
        near_kernel,
        (shape((length, width), F32), shape((length, HEAD_DIM), F32)),
        (x_own, core, far),
        "near_rows",
    )
    grad_keys, give, keep, gterm, _, _ = call(
        functools.partial(attention_kernel, near),
        (
            shape((1, length, width), BF),
            shape((2 * SLAB, width), BF),
            shape((2 * SLAB, width), F32),
            shape((near, NH, HEAD_DIM), BF),
            shape((length, width), F32),
            shape((length, HEAD_DIM), F32),
        ),
        (x_near, rs_near, farcore, keys, grad_out, gains),
        "attention_backward",
        hbm_out=(0, 3),
        alias={0: 4, 1: 5},
        scratch=[
            pltpu.VMEM((near, NH, HEAD_DIM), BF),
            pltpu.SemaphoreType.DMA((1,)),
            pltpu.VMEM((length, width), F32),
            pltpu.VMEM((length, HEAD_DIM), F32),
            pltpu.VMEM((NH, HEAD_DIM), F32),
            pltpu.VMEM((HEAD_DIM, HEAD_DIM), F32),
            pltpu.VMEM((length - HEAD_DIM, length - HEAD_DIM), F32),
            pltpu.VMEM((1, length, width), BF),
            pltpu.SemaphoreType.DMA((NH // SENT,)),
        ],
        cost=(10 * length * length * width, 16 << 20),
    )
    got = swap(give, 1)
    mine, send = call(
        between_kernel, (shape((SLAB, width), F32), shape((part, width), BF)), (keep, got), "add_core", cost=(0, 0)
    )
    last = swap(send, 2)
    first = lax.all_to_all(gterm, "y", 0, 0, tiled=True)
    (wide,) = call(
        functools.partial(spread_kernel, rest),
        (shape((rest, NH, HEAD_DIM), BF),),
        (first,),
        "sum_near",
        cost=(8 << 30, 0),
    )
    second = lax.all_to_all(wide, ("zh", "x"), 0, 0, tiled=True)
    grad_trunk, grad_gains = call(
        final_kernel, (shape((part, width), BF), shape((1, width), F32)), (mine, last, second), "add_far"
    )
    return grad_trunk, grad_keys, grad_gains


def solution(mesh):
    dp = mesh.shape["dp"]
    near = min(dp, 4)
    zh = 4 if dp >= 16 else 1
    y = dp // near // zh
    fine = Mesh(mesh.devices.reshape(y, zh, near, 2, 2), ("y", "zh", "x", "zl", "core"))
    dps = ("y", "zh", "x")
    return jax.shard_map(
        functools.partial(on_device, y, zh * near),
        mesh=fine,
        in_specs=(
            P(dps + HEAD, None),
            P(HEAD, dps, None),
            P(HEAD, None),
            P(HEAD, dps, None),
        ),
        out_specs=(P(dps + HEAD, None), P(HEAD, dps, None), P(HEAD, None)),
        check_vma=False,
    )
```
